32 devices in a mesh: grp: 2 (over x), dom: 16 (over z, y, core).
Axes of the slice: x: 2, y: 2, z: 4, core: 2. Of those that a mesh axis runs over, the one named last changes fastest.
Arguments:
- conn: int32 [2, 16, 27, 512], P('grp', 'dom'), may hold values from 0 to 5119, as said below
- live: int32 [2, 16, 512], P('grp', 'dom'), may hold values from 0 to 1, as said below
- stiffness: float32 [2, 16, 512], P('grp', 'dom'), may hold values from 1 to 10
- owner: int32 [2, 16, 5120], P('grp', 'dom'), may hold values from 0 to 1, as said below
- free: int32 [2, 16, 5120], P('grp', 'dom'), may hold values from 0 to 1, as said below
- x_faces: int32 [2, 16, 2, 384], P('grp', 'dom'), may hold values from 0 to 5119, as said below
- peer_table: int32 [2, 256, 640], P('grp', 'dom'), may hold values from 0 to 5119, as said below
- disp: float32 [2, 16, 3, 5120], P('grp', 'dom'), may hold values from -0.024 to 0.024
- load: float32 [2, 16, 3, 5120], P('grp', 'dom'), may hold values from -15 to 15
Outputs:
- update: float32 [2, 16, 3, 5120], P('grp', 'dom')
- residual: float32 [2, 16, 3, 5120], P('grp', 'dom')
The draws below stay inside these ranges and needn't reach their ends.
Inputs may be any that keep to these rules, and one draw needn't show every extreme that they name: `conn`: for a live slot the column lists the local ids of the element's 27 nodes, node a at offset (a // 9, a // 3 % 3, a % 3) half-sides from the element's lowest corner along (x, y, z); elements fill each device's box of 8 x 16 x 4 cubes, and the boxes tile the specimen, grp index along x, dom index = 8 * (box along y) + (box along z). A padded slot lists 5120 - 1, an id that is no node. Live slots come before padded ones on every device; some device has all 512 slots live. `owner`: exactly one copy of every mesh node has 1; ids that are no node have 0. `free`: 1 exactly on nodes that touch a live element and do not lie on the face x = 0 of the specimen, equal on all copies of a node; 0 on ids that are no node. `x_faces`: row 1 of a device and row 0 of the device with the next grp index and the same dom index list the same nodes in the same order; padding is 5119. `peer_table`: row q of device p and row p of device q (same grp index) list the nodes the two boxes share, in the same order, padded with 5119; a row is all padding unless the dom indices differ by 1, 7, 8 or 9.
All inputs are finite; a program needn't handle non-finite values.
Results may differ from the reference program's by a relative error of at most 0.00011.
Values sent between devices are 32-bit elements; how exact they have to be, the bound alone decides.
A program may use at most 128 MiB of HBM per device.

```python
import math
import jax
import jax.numpy as jnp
import numpy as np
from jax import lax

BX = 8
BY = 16
BZ = 4
PZ = 8
ITERS = 2
PY = 2
ELEMS = 512
NODES = 5049
SLOTS = 5120
PEER_WIDTH = 640
FACE_WIDTH = 384
N_GRP = 2
N_DOM = 16


def element_nodes():
    span_y = 2 * BY + 1
    span_z = 2 * BZ + 1
    corner_x, corner_y, corner_z = np.meshgrid(np.arange(BX), np.arange(BY), np.arange(BZ), indexing='ij')
    offset = np.arange(27)
    node_x = 2 * corner_x.reshape(-1, 1) + offset // 9
    node_y = 2 * corner_y.reshape(-1, 1) + offset // 3 % 3
    node_z = 2 * corner_z.reshape(-1, 1) + offset % 3
    return (node_x * span_y + node_y) * span_z + node_z


def padded_list(indices, width):
    return np.concatenate([indices, np.full(width - indices.shape[0], NODES)]).astype(np.int32)


def shared_lists():
    span_x, span_y, span_z = (2 * BX + 1, 2 * BY + 1, 2 * BZ + 1)
    node_grid = np.arange(NODES).reshape(span_x, span_y, span_z)
    listing = []
    for step_y in (-1, 0, 1):
        for step_z in (-1, 0, 1):
            if step_y == 0 and step_z == 0:
                continue
            picked_y = np.arange(span_y) if step_y == 0 else np.array([0 if step_y < 0 else span_y - 1])
            picked_z = np.arange(span_z) if step_z == 0 else np.array([0 if step_z < 0 else span_z - 1])
            picked = node_grid[:, picked_y, :][:, :, picked_z].reshape(-1)
            listing.append((step_y, step_z, padded_list(picked, PEER_WIDTH)))
    return listing


def shuffle_slots(device_key):
    return jax.random.permutation(device_key, SLOTS - 1).astype(jnp.int32)


def shuffle_elements(device_key):
    return jax.random.permutation(device_key, ELEMS).astype(jnp.int32)


def mesh_layout(key):
    level_key, fullest_key, cell_key, number_key, ordering_key = jax.random.split(key, 5)
    devices = N_GRP * N_DOM
    levels = jax.random.randint(level_key, (devices,), 4, 10)
    fullest = jax.random.randint(fullest_key, (), 0, devices)
    levels = jnp.where(jnp.arange(devices) == fullest, 10, levels).reshape(N_GRP, PY, PZ)
    cell_draws = jax.random.randint(cell_key, (N_GRP * BX, PY * BY, PZ * BZ), 0, 10)
    thresholds = jnp.repeat(jnp.repeat(jnp.repeat(levels, BX, 0), BY, 1), BZ, 2)
    live_grid = (cell_draws < thresholds).astype(jnp.int32)
    touched = live_grid
    for dimension in range(3):
        number = touched.shape[dimension]
        widened = jnp.pad(touched, [(1, 1) if other == dimension else (0, 0) for other in range(3)])
        node_index = np.arange(2 * number + 1)
        touched = jnp.maximum(jnp.take(widened, node_index // 2 + 1, axis=dimension), jnp.take(widened, (node_index + 1) // 2, axis=dimension))
    span_x, span_y, span_z = (2 * BX + 1, 2 * BY + 1, 2 * BZ + 1)
    along_x = (2 * BX * jnp.arange(N_GRP))[:, None] + jnp.arange(span_x)[None, :]
    along_y = (2 * BY * jnp.arange(PY))[:, None] + jnp.arange(span_y)[None, :]
    along_z = (2 * BZ * jnp.arange(PZ))[:, None] + jnp.arange(span_z)[None, :]
    local_touch = touched[along_x[:, None, None, :, None, None], along_y[None, :, None, None, :, None], along_z[None, None, :, None, None, :]]
    local_touch = local_touch.reshape(devices, NODES)
    local_live = live_grid.reshape(N_GRP, BX, PY, BY, PZ, BZ).transpose(0, 2, 4, 1, 3, 5).reshape(devices, ELEMS)
    device_grp = jnp.arange(devices) // N_DOM
    device_dom = jnp.arange(devices) % N_DOM
    device_py = device_dom // PZ
    device_pz = device_dom % PZ
    position = np.arange(NODES)
    position_x = jnp.asarray(position // (span_y * span_z))[None, :]
    position_y = jnp.asarray(position // span_z % span_y)[None, :]
    position_z = jnp.asarray(position % span_z)[None, :]
    owned_nodes = jnp.logical_not((position_x == 0) & (device_grp[:, None] > 0))
    owned_nodes = owned_nodes & jnp.logical_not((position_y == 0) & (device_py[:, None] > 0))
    owned_nodes = owned_nodes & jnp.logical_not((position_z == 0) & (device_pz[:, None] > 0))
    free_nodes = (local_touch > 0) & jnp.logical_not((position_x == 0) & (device_grp[:, None] == 0))
    numbering = jax.vmap(shuffle_slots)(jax.random.split(number_key, devices))[:, :NODES]
    extended = jnp.concatenate([numbering, jnp.full((devices, 1), SLOTS - 1, jnp.int32)], axis=1)
    device_rows = jnp.arange(devices)[:, None]
    owner_local = jnp.zeros((devices, SLOTS), jnp.int32).at[device_rows, numbering].set(owned_nodes.astype(jnp.int32))
    free_local = jnp.zeros((devices, SLOTS), jnp.int32).at[device_rows, numbering].set(free_nodes.astype(jnp.int32))
    rankings = jax.vmap(shuffle_elements)(jax.random.split(ordering_key, devices))
    scores = (1 - local_live) * ELEMS + rankings
    ordering = jnp.argsort(scores, axis=1, stable=True)
    live_sorted = jnp.take_along_axis(local_live, ordering, axis=1)
    element_table = jnp.asarray(element_nodes().astype(np.int32))
    structured = element_table[ordering]
    node_ids = jnp.take_along_axis(numbering, structured.reshape(devices, -1), axis=1).reshape(devices, ELEMS, 27)
    connect = jnp.where(live_sorted[:, :, None] > 0, node_ids, SLOTS - 1).transpose(0, 2, 1)
    node_grid = np.arange(NODES).reshape(span_x, span_y, span_z)
    lower_face = padded_list(node_grid[0].reshape(-1), FACE_WIDTH)
    upper_face = padded_list(node_grid[-1].reshape(-1), FACE_WIDTH)
    faces = jnp.stack([jnp.take(extended, jnp.asarray(lower_face), axis=1), jnp.take(extended, jnp.asarray(upper_face), axis=1)], axis=1)
    table = jnp.full((devices, N_DOM, PEER_WIDTH), SLOTS - 1, jnp.int32)
    for step_y, step_z, listing in shared_lists():
        rows = jnp.take(extended, jnp.asarray(listing), axis=1)
        valid = (device_py + step_y >= 0) & (device_py + step_y < PY) & (device_pz + step_z >= 0) & (device_pz + step_z < PZ)
        target = jnp.where(valid, device_dom + step_y * PZ + step_z, device_dom)
        table = table.at[jnp.arange(devices), target].set(jnp.where(valid[:, None], rows, SLOTS - 1))
    return {'conn': connect.reshape(N_GRP, N_DOM, 27, ELEMS), 'live': live_sorted.reshape(N_GRP, N_DOM, ELEMS), 'owner': owner_local.reshape(N_GRP, N_DOM, SLOTS), 'free': free_local.reshape(N_GRP, N_DOM, SLOTS), 'faces': faces.reshape(N_GRP, N_DOM, 2, FACE_WIDTH), 'table': table.reshape(N_GRP, N_DOM * N_DOM, PEER_WIDTH)}


def draw_conn(key, part):
    return mesh_layout(key)['conn']


def draw_live(key, part):
    return mesh_layout(key)['live']


def draw_owner(key, part):
    return mesh_layout(key)['owner']


def draw_free(key, part):
    return mesh_layout(key)['free']


def draw_x_faces(key, part):
    return mesh_layout(key)['faces']


def draw_peer_table(key, part):
    return mesh_layout(key)['table']


def draw_load(key, part):
    key = jax.random.fold_in(key, 7)
    devices = N_GRP * N_DOM
    ramp = 1.0 + 2.0 * jnp.arange(devices, dtype=jnp.float32).reshape(N_GRP, N_DOM, 1, 1) / max(devices - 1, 1)
    normal_draw = jnp.clip(jax.random.normal(key, (N_GRP, N_DOM, 3, SLOTS), jnp.float32), -5.0, 5.0)
    result = normal_draw * ramp
    return result


def block_levels(stream_key, shape, cuts, least, largest):
    loudness, own = 1.0, jax.random.fold_in(stream_key, 6)
    for dim, shards_of in cuts:
        steps = jnp.exp(jax.random.uniform(jax.random.fold_in(own, dim), (shards_of,), jnp.float32, least / len(cuts), largest / len(cuts)))
        loudness = loudness * jnp.repeat(steps, shape[dim] // shards_of).reshape([-1 if axis == dim else 1 for axis in range(len(shape))])
    return loudness


def scatter_about(key, dims, scale, bound, cuts=(), kind=jnp.bfloat16):
    gain = block_levels(key, dims, cuts, -0.22, 0.18) if cuts else 1.0
    drawn = jax.random.normal(key, dims, jnp.float32) * scale * gain
    return jnp.minimum(jnp.maximum(drawn, -bound), bound).astype(kind)


def setup_inputs(seed: int = 0) -> dict:
    seeds = jax.random.split(jax.random.key(seed), 10)
    return {
        "conn": draw_conn(jax.random.fold_in(seeds[9], 71), 0),
        "live": draw_live(jax.random.fold_in(seeds[9], 71), 0),
        "stiffness": jnp.clip(jnp.exp(math.log(10.0) - 2.3025851 * jax.random.uniform(seeds[2], (N_GRP, N_DOM, ELEMS), jnp.float32) ** block_levels(seeds[2], (N_GRP, N_DOM, ELEMS), ((0, 2), (1, 16)), -0.2, 0.2)), 1.0, 10.0),
        "owner": draw_owner(jax.random.fold_in(seeds[9], 71), 0),
        "free": draw_free(jax.random.fold_in(seeds[9], 71), 0),
        "x_faces": draw_x_faces(jax.random.fold_in(seeds[9], 71), 0),
        "peer_table": draw_peer_table(jax.random.fold_in(seeds[9], 71), 0),
        "disp": scatter_about(seeds[7], (N_GRP, N_DOM, 3, SLOTS), 0.006, 0.024, ((0, 2), (1, 16)), jnp.float32),
        "load": draw_load(jax.random.fold_in(seeds[9], 71), 0),
    }


def lagrange_values(place):
    return np.array([place * (place - 1.0) / 2.0, 1.0 - place * place, place * (place + 1.0) / 2.0])

def lagrange_slopes(place):
    return np.array([place - 0.5, -2.0 * place, place + 0.5])

def basis_tables():
    points = [-math.sqrt(0.6), 0.0, math.sqrt(0.6)]
    weights = [5.0 / 9.0, 8.0 / 9.0, 5.0 / 9.0]
    values = np.stack([lagrange_values(place) for place in points])
    slopes = np.stack([lagrange_slopes(place) for place in points])
    gradient_table = np.zeros((3, 27, 27))
    quad_weight = np.zeros(27)
    for point_index in range(27):
        first, second, third = (point_index // 9, point_index // 3 % 3, point_index % 3)
        quad_weight[point_index] = weights[first] * weights[second] * weights[third]
        for node_index in range(27):
            along_x, along_y, along_z = (node_index // 9, node_index // 3 % 3, node_index % 3)
            gradient_table[0, point_index, node_index] = slopes[first, along_x] * values[second, along_y] * values[third, along_z]
            gradient_table[1, point_index, node_index] = values[first, along_x] * slopes[second, along_y] * values[third, along_z]
            gradient_table[2, point_index, node_index] = values[first, along_x] * values[second, along_y] * slopes[third, along_z]
    return (jnp.asarray(gradient_table.reshape(81, 27), jnp.float32), jnp.asarray(quad_weight.reshape(27, 1), jnp.float32))

def element_terms(gradient_table, quad_weight, nodal_state, nodal_probe, shear_modulus, lame_first, tangent):
    block_size = nodal_state.shape[2]
    identity = jnp.eye(3, dtype=jnp.float32)[:, :, None, None]
    deform = identity + jnp.einsum('ma,cab->cmb', gradient_table, nodal_state, precision=lax.Precision.HIGHEST).reshape(3, 3, 27, block_size)
    volume = lax.optimization_barrier(jnp.sum(deform[0] * jnp.cross(deform[1], deform[2], axis=0), axis=0))
    inverse = jnp.stack([jnp.cross(deform[1], deform[2], axis=0), jnp.cross(deform[2], deform[0], axis=0), jnp.cross(deform[0], deform[1], axis=0)], axis=1) / volume
    inverse_t = jnp.swapaxes(inverse, 0, 1)
    log_volume = jnp.log(volume)
    if tangent:
        change = jnp.einsum('ma,cab->cmb', gradient_table, nodal_probe, precision=lax.Precision.HIGHEST).reshape(3, 3, 27, block_size)
        product = lax.optimization_barrier(jnp.sum(inverse[:, :, None] * change[None], axis=1))
        twisted = lax.optimization_barrier(jnp.sum(product[:, :, None] * inverse[None], axis=1))
        trace_term = product[0, 0] + product[1, 1] + product[2, 2]
        stress = shear_modulus * change + (shear_modulus - lame_first * log_volume) * jnp.swapaxes(twisted, 0, 1) + lame_first * trace_term * inverse_t
    else:
        stress = shear_modulus * (deform - inverse_t) + lame_first * log_volume * inverse_t
    weighted = (stress * quad_weight).reshape(3, 81, block_size)
    return jnp.einsum('ma,cmb->cab', gradient_table, weighted, precision=lax.Precision.HIGHEST)

def local_forces(gradient_table, quad_weight, connect, shear_modulus, lame_first, state_field, probe_field, tangent, block_count):
    block_size = min(connect.shape[1], 512)

    def accumulate(block_index, summed_force):
        first_slot = block_index * block_size
        node_ids = lax.dynamic_slice_in_dim(connect, first_slot, block_size, 1)
        shear_block = lax.dynamic_slice_in_dim(shear_modulus, first_slot, block_size, 0)
        lame_block = lax.dynamic_slice_in_dim(lame_first, first_slot, block_size, 0)
        contribution = element_terms(gradient_table, quad_weight, state_field[:, node_ids], probe_field[:, node_ids], shear_block, lame_block, tangent)
        return summed_force.at[:, node_ids].add(contribution)
    return lax.fori_loop(0, block_count, accumulate, jnp.zeros(state_field.shape, jnp.float32))

def add_entries(values_field, node_ids, extra_values):
    return values_field.at[:, node_ids].add(extra_values)

def assemble(field, x_faces, peer_table):
    lower_ids = x_faces[:, :, 0]
    upper_ids = x_faces[:, :, 1]
    up_values = jnp.take_along_axis(field, upper_ids[:, :, None, :], axis=3)
    down_values = jnp.take_along_axis(field, lower_ids[:, :, None, :], axis=3)
    from_below = jnp.concatenate([jnp.zeros_like(up_values[:1]), up_values[:-1]], axis=0)
    from_above = jnp.concatenate([down_values[1:], jnp.zeros_like(down_values[:1])], axis=0)
    adder = jax.vmap(jax.vmap(add_entries))
    summed = adder(adder(field, lower_ids, from_below), upper_ids, from_above)
    peer_rows = peer_table.reshape(N_GRP, N_DOM, N_DOM, peer_table.shape[2])

    def receive(receiver):
        sender_rows = lax.dynamic_index_in_dim(peer_rows, receiver, 2, keepdims=False)
        sent_values = jnp.take_along_axis(summed, sender_rows[:, :, None, :], axis=3)
        own_rows = lax.dynamic_index_in_dim(peer_rows, receiver, 1, keepdims=False)
        own_field = lax.dynamic_index_in_dim(summed, receiver, 1, keepdims=False)

        def add_group(values_field, node_ids, extra_values):
            return values_field.at[:, node_ids.reshape(-1)].add(jnp.swapaxes(extra_values, 0, 1).reshape(3, -1))
        return jax.vmap(add_group)(own_field, own_rows, sent_values)
    result = lax.map(receive, jnp.arange(N_DOM))
    return jnp.swapaxes(result, 0, 1)

def reference(conn, live, stiffness, owner, free, x_faces, peer_table, disp, load):
    gradient_table, quad_weight = basis_tables()
    devices = N_GRP * N_DOM
    owner_weight = owner.astype(jnp.float32)[:, :, None, :]
    free_weight = free.astype(jnp.float32)[:, :, None, :]
    live_weight = live.astype(jnp.float32)
    shear_modulus = live_weight * stiffness / 2.6
    lame_first = live_weight * stiffness * 0.3 / 0.52
    block_count = conn.shape[3] // min(conn.shape[3], 512)

    def flatten(stacked):
        return stacked.reshape((devices,) + stacked.shape[2:])

    def forces(state_field, probe_field, tangent):

        def one_device(operands):
            connect, shear_one, lame_one, state_one, probe_one = operands
            return local_forces(gradient_table, quad_weight, connect, shear_one, lame_one, state_one, probe_one, tangent, block_count)
        result = lax.map(one_device, (flatten(conn), flatten(shear_modulus), flatten(lame_first), flatten(state_field), flatten(probe_field)))
        return result.reshape(state_field.shape)

    def inner_product(first_field, second_field):
        return jnp.sum(owner_weight * first_field * second_field)
    state_field = assemble(owner_weight * disp, x_faces, peer_table)
    internal_force = forces(state_field, state_field, False)
    right_side = free_weight * assemble(owner_weight * load - internal_force, x_faces, peer_table)

    def operator(field):
        return free_weight * assemble(forces(state_field, field, True), x_faces, peer_table)
    solution = jnp.zeros_like(right_side)
    residual = right_side
    direction = right_side
    norm_now = inner_product(residual, residual)
    for iteration in range(ITERS):
        image_field = operator(direction)
        step_length = norm_now / inner_product(direction, image_field)
        solution = solution + step_length * direction
        residual = residual - step_length * image_field
        if iteration + 1 < ITERS:
            norm_next = inner_product(residual, residual)
            direction = residual + norm_next / norm_now * direction
            norm_now = norm_next
    return (solution, residual)
```

```python
import functools
import math

import jax
import jax.numpy as jnp
import numpy as np
from jax import lax
from jax.experimental import pallas as pl
from jax.experimental.pallas import tpu as pltpu
from jax.sharding import PartitionSpec as P

MESH = pl.DeviceIdType.MESH
PZ = 8
LANES = 128
Q = 32
F32 = jnp.float32
BF16 = jnp.bfloat16
DIRECTIONS = (
    (0, -1, 640), (0, 1, 640), (-1, 0, 256), (1, 0, 256),
    (-1, -1, 128), (1, 1, 128), (-1, 1, 128), (1, -1, 128),
)
OPPOSITE = (1, 0, 3, 2, 5, 4, 7, 6)
STARTS = tuple(int(s) for s in np.cumsum([0] + [w for _, _, w in DIRECTIONS]))
DOM_WIDTH = STARTS[-1]


def lagrange_values(place):
    return np.array([place * (place - 1.0) / 2.0, 1.0 - place * place, place * (place + 1.0) / 2.0])


def lagrange_slopes(place):
    return np.array([place - 0.5, -2.0 * place, place + 0.5])


def basis_tables():
    points = [-math.sqrt(0.6), 0.0, math.sqrt(0.6)]
    weights = np.array([5.0 / 9.0, 8.0 / 9.0, 5.0 / 9.0])
    values = np.stack([lagrange_values(place) for place in points])
    slopes = np.stack([lagrange_slopes(place) for place in points])
    table = np.zeros((3, Q, Q))
    for d in range(3):
        factors = [slopes if d == k else values for k in range(3)]
        table[d, :27, :27] = np.einsum("ax,by,cz->abcxyz", *factors).reshape(27, 27)
    weight = np.einsum("a,b,c->abc", weights, weights, weights).reshape(27)
    forward = table.reshape(3 * Q, Q).copy()
    table[:, :27] *= weight[None, :, None]
    return forward, table.reshape(3 * Q, Q).T


def three_terms(table):
    table = np.asarray(table, np.float32)
    high = table.astype(BF16)
    low = (table - high.astype(np.float32)).astype(BF16)
    return jnp.asarray(np.concatenate([high, low, high], axis=1))


def halves(value):
    high = value.astype(BF16).astype(F32)
    return high, value - high


def stacked_halves(value):
    high, low = halves(value)
    return jnp.concatenate([high, low], axis=0).astype(BF16)


def one_hot(ids):
    spot = lax.broadcasted_iota(jnp.int32, (LANES, ids.shape[1]), 0)
    return jnp.where(spot == (ids & (LANES - 1)), 1.0, 0.0).astype(BF16)


def row_mask(ids, rows):
    spot = lax.broadcasted_iota(jnp.int32, (rows, ids.shape[1]), 0)
    return spot == (ids >> 7)


def pick(split_field, hot, ids):
    wide = jnp.dot(split_field, hot, preferred_element_type=F32)
    half = wide.shape[0] // 2
    wide = wide[:half] + wide[half:]
    rows = half // 3
    mask = row_mask(ids, rows)
    return [
        jnp.sum(jnp.where(mask, wide[c * rows : (c + 1) * rows], 0.0), axis=0, keepdims=True)
        for c in range(3)
    ]


def spread(values, hot, ids, rows):
    mask = row_mask(ids, rows)
    parts = [halves(value) for value in values]
    tall = jnp.concatenate([jnp.where(mask, parts[c][s], 0.0) for s in range(2) for c in range(3)], axis=0)
    total = lax.dot_general(
        tall.astype(BF16), hot, (((1,), (1,)), ((), ())), preferred_element_type=F32
    )
    return total


def cross(one, two):
    return [
        one[1] * two[2] - one[2] * two[1],
        one[2] * two[0] - one[0] * two[2],
        one[0] * two[1] - one[1] * two[0],
    ]


def kernel(
    n_grp, n_dom,
    conn, live, stiff, owner, free, faces, peers, disp, load, fwd, rev,
    update, residual,
    hot_e, hot_x, hot_d, ids_x, ids_d, nodal, inverse, coef, force,
    send_x, recv_x, send_d, recv_d, dot_send, dot_dom, dot_grp,
    sx, rx, sd, rd, s_dot, r_dot, s_grp, r_grp,
):
    grp, dom = lax.axis_index("grp"), lax.axis_index("dom")
    py, pz = dom // PZ, lax.rem(dom, PZ)
    n_py = n_dom // PZ
    rows = owner.shape[0]
    slots = conn.shape[1]

    def exists(way):
        sy, sz, _ = DIRECTIONS[way]
        return (py + sy >= 0) & (py + sy < n_py) & (pz + sz >= 0) & (pz + sz < PZ)

    def peer(way):
        sy, sz, _ = DIRECTIONS[way]
        return jnp.clip(dom + sy * PZ + sz, 0, n_dom - 1)

    recv_x[...] = jnp.zeros_like(recv_x)
    recv_d[...] = jnp.zeros_like(recv_d)
    send_x[...] = jnp.zeros_like(send_x)
    send_d[...] = jnp.zeros_like(send_d)

    barrier = pltpu.get_barrier_semaphore()
    for k in range(1, n_dom):
        pl.semaphore_signal(barrier, inc=1, device_id={"dom": lax.rem(dom + k, n_dom)}, device_id_type=MESH)
    for k in range(1, n_grp):
        pl.semaphore_signal(barrier, inc=1, device_id={"grp": lax.rem(grp + k, n_grp)}, device_id_type=MESH)

    width_x = faces.shape[1]
    for side in range(2):
        ids_x[:, side * width_x : (side + 1) * width_x] = faces[side : side + 1, :]
    for way, (_, _, width) in enumerate(DIRECTIONS):
        ids_d[:, STARTS[way] : STARTS[way + 1]] = peers[pl.ds(peer(way), 1), :][:, :width]
    hot_x[...] = one_hot(ids_x[...])
    hot_d[...] = one_hot(ids_d[...])

    @pl.loop(0, 27)
    def _(a):
        hot_e[a] = one_hot(conn[pl.ds(a, 1), :])

    nodal[...] = jnp.zeros_like(nodal)
    own = jnp.concatenate([owner[...].astype(F32)] * 3, axis=0)
    loose = jnp.concatenate([free[...].astype(F32)] * 3, axis=0)
    alive = live[...].astype(F32)
    shear = alive * stiff[...] / 2.6
    lame = alive * stiff[...] * 0.3 / 0.52

    pl.semaphore_wait(barrier, n_dom - 1 + n_grp - 1)

    def copy_x(turn, side):
        there = 1 - side
        return pltpu.make_async_remote_copy(
            src_ref=send_x.at[turn, :, pl.ds(side * width_x, width_x)],
            dst_ref=recv_x.at[turn, :, pl.ds(there * width_x, width_x)],
            send_sem=sx.at[turn, side],
            recv_sem=rx.at[turn, there],
            device_id={"grp": jnp.clip(grp + 2 * side - 1, 0, n_grp - 1)},
            device_id_type=MESH,
        )

    def copy_d(turn, way):
        there = OPPOSITE[way]
        width = DIRECTIONS[way][2]
        return pltpu.make_async_remote_copy(
            src_ref=send_d.at[turn, :, pl.ds(STARTS[way], width)],
            dst_ref=recv_d.at[turn, :, pl.ds(STARTS[there], width)],
            send_sem=sd.at[turn, way],
            recv_sem=rd.at[turn, there],
            device_id={"dom": peer(way)},
            device_id_type=MESH,
        )

    has_x = (grp > 0, grp < n_grp - 1)

    def added(total):
        half = total.shape[0] // 2
        return total[:half] + total[half:]

    def assemble(field, turn, between_x=None, between_d=None):
        picked = pick(stacked_halves(field), hot_x[...], ids_x[...])
        for c in range(3):
            send_x[turn, c : c + 1, :] = picked[c]
        for side in range(2):
            @pl.when(has_x[side])
            def _():
                copy_x(turn, side).start()
        if between_x is not None:
            between_x()
        for side in range(2):
            @pl.when(has_x[side])
            def _():
                copy_x(turn, side).wait_send()
                copy_x(turn, 1 - side).wait_recv()
        got = [recv_x[turn, c : c + 1, :] for c in range(3)]
        field = field + added(spread(got, hot_x[...], ids_x[...], rows))
        picked = pick(stacked_halves(field), hot_d[...], ids_d[...])
        for c in range(3):
            send_d[turn, c : c + 1, :] = picked[c]
        for way in range(8):
            @pl.when(exists(way))
            def _():
                copy_d(turn, way).start()
        if between_d is not None:
            between_d()
        for way in range(8):
            @pl.when(exists(way))
            def _():
                copy_d(turn, way).wait_send()
                copy_d(turn, OPPOSITE[way]).wait_recv()
        got = [recv_d[turn, c : c + 1, :] for c in range(3)]
        return field + added(spread(got, hot_d[...], ids_d[...], rows))

    def gradients(at):
        result = []
        for c in range(3):
            high, low = halves(nodal[c, :, at])
            stack = jnp.concatenate([high, high, low], axis=0).astype(BF16)
            full = jnp.dot(fwd[...], stack, preferred_element_type=F32)
            result.append([full[d * Q : (d + 1) * Q] for d in range(3)])
        return result

    def forces(field, tangent):
        split_field = stacked_halves(field)

        @pl.loop(0, 9)
        def _(step):
            for part in range(3):
                a = step * 3 + part
                picked = pick(split_field, hot_e[a], conn[pl.ds(a, 1), :])
                for c in range(3):
                    nodal[c, pl.ds(a, 1), :] = picked[c]

        for first in range(0, slots, LANES):
            at = slice(first, first + LANES)
            mu, lam = shear[:, at], lame[:, at]
            change = gradients(at)
            if tangent:
                inv = [[inverse[3 * i + j, :, at] for j in range(3)] for i in range(3)]
                twist = coef[:, at]
                product = [
                    [sum(inv[i][k] * change[k][j] for k in range(3)) for j in range(3)] for i in range(3)
                ]
                trace = lam * (product[0][0] + product[1][1] + product[2][2])
                stress = [
                    [
                        mu * change[c][d]
                        + twist * sum(product[d][k] * inv[k][c] for k in range(3))
                        + trace * inv[d][c]
                        for d in range(3)
                    ]
                    for c in range(3)
                ]
            else:
                deform = [[change[c][d] + (1.0 if c == d else 0.0) for d in range(3)] for c in range(3)]
                columns = [
                    cross(deform[1], deform[2]), cross(deform[2], deform[0]), cross(deform[0], deform[1])
                ]
                volume = sum(deform[0][i] * columns[0][i] for i in range(3))
                over = 1.0 / volume
                logged = lam * jnp.log(volume)
                twist = mu - logged
                coef[:, at] = twist
                inv = [[columns[j][i] * over for j in range(3)] for i in range(3)]
                for i in range(3):
                    for j in range(3):
                        inverse[3 * i + j, :, at] = inv[i][j]
                stress = [[mu * deform[c][d] - twist * inv[d][c] for d in range(3)] for c in range(3)]
            for c in range(3):
                tall = jnp.concatenate(stress[c], axis=0)
                high, low = halves(tall)
                stack = jnp.concatenate([high, high, low], axis=0).astype(BF16)
                force[c, :, at] = jnp.dot(rev[...], stack, preferred_element_type=F32)

        def body(step, total):
            for part in range(3):
                a = step * 3 + part
                values = [force[c, pl.ds(a, 1), :] for c in range(3)]
                total = total + spread(values, hot_e[a], conn[pl.ds(a, 1), :], rows)
            return total

        return added(lax.fori_loop(0, 9, body, jnp.zeros((6 * rows, LANES), F32)))

    state = assemble(own * disp[...], 0)
    inner = forces(state, False)
    right = loose * assemble(own * load[...] - inner, 1)
    image = loose * assemble(forces(right, True), 2)
    second = forces(image, True)

    def lanes(value):
        return jnp.sum(value, axis=0, keepdims=True)

    partial = [
        lanes(own * right * right), lanes(own * right * image),
        lanes(own * image * image), lanes(image * second),
    ]
    dot_send[0] = jnp.concatenate(partial + [jnp.zeros((4, LANES), F32)], axis=0)

    def dot_copy(k):
        return pltpu.make_async_remote_copy(
            src_ref=dot_send.at[0], dst_ref=dot_dom.at[k], send_sem=s_dot.at[k], recv_sem=r_dot.at[k],
            device_id={"dom": lax.rem(dom + k, n_dom)}, device_id_type=MESH,
        )

    def grp_copy(k):
        return pltpu.make_async_remote_copy(
            src_ref=dot_send.at[1], dst_ref=dot_grp.at[k], send_sem=s_grp.at[k], recv_sem=r_grp.at[k],
            device_id={"grp": lax.rem(grp + k, n_grp)}, device_id_type=MESH,
        )

    def start_dots():
        for k in range(1, n_dom):
            dot_copy(k).start()

    def middle_dots():
        total = dot_send[0]
        for k in range(1, n_dom):
            dot_copy(k).wait()
            total = total + dot_dom[k]
        dot_send[1] = total
        for k in range(1, n_grp):
            grp_copy(k).start()

    outer = loose * assemble(second, 3, start_dots, middle_dots)
    total = dot_send[1]
    for k in range(1, n_grp):
        grp_copy(k).wait()
        total = total + dot_grp[k]
    sums = jnp.sum(total, axis=1, keepdims=True)
    rr, rq, qq, qu = (sums[k : k + 1] for k in range(4))
    step = rr / rq
    later = step * step * qq - rr
    ratio = later / rr
    grown = 1.0 + ratio
    curve = grown * grown * rq - 2.0 * grown * step * qq + step * step * qu
    last = later / curve
    moved = right - step * image
    direction = moved + ratio * right
    update[...] = step * right + last * direction
    residual[...] = moved - last * (grown * image - step * outer)


def per_device(n_grp, n_dom, conn, live, stiffness, owner, free, x_faces, peer_table, disp, load):
    slots = conn.shape[3]
    rows = owner.shape[2] // LANES
    width_x = x_faces.shape[3]
    forward, backward = basis_tables()
    vmem = pl.BlockSpec(memory_space=pltpu.VMEM)
    shape = jax.ShapeDtypeStruct((3 * rows, LANES), F32)
    dma = pltpu.SemaphoreType.DMA
    update, residual = pl.pallas_call(
        functools.partial(kernel, n_grp, n_dom),
        out_shape=(shape, shape),
        in_specs=[vmem] * 11,
        out_specs=(vmem, vmem),
        scratch_shapes=[
            pltpu.VMEM((27, LANES, slots), BF16),
            pltpu.VMEM((LANES, 2 * width_x), BF16),
            pltpu.VMEM((LANES, DOM_WIDTH), BF16),
            pltpu.VMEM((1, 2 * width_x), jnp.int32),
            pltpu.VMEM((1, DOM_WIDTH), jnp.int32),
            pltpu.VMEM((3, Q, slots), F32),
            pltpu.VMEM((9, Q, slots), F32),
            pltpu.VMEM((Q, slots), F32),
            pltpu.VMEM((3, Q, slots), F32),
            pltpu.VMEM((4, 8, 2 * width_x), F32),
            pltpu.VMEM((4, 8, 2 * width_x), F32),
            pltpu.VMEM((4, 8, DOM_WIDTH), F32),
            pltpu.VMEM((4, 8, DOM_WIDTH), F32),
            pltpu.VMEM((2, 8, LANES), F32),
            pltpu.VMEM((n_dom, 8, LANES), F32),
            pltpu.VMEM((n_grp, 8, LANES), F32),
            dma((4, 2)), dma((4, 2)), dma((4, 8)), dma((4, 8)),
            dma((n_dom,)), dma((n_dom,)), dma((n_grp,)), dma((n_grp,)),
        ],
        compiler_params=pltpu.CompilerParams(
            collective_id=0, has_side_effects=True, vmem_limit_bytes=48 * 1024 * 1024
        ),
        cost_estimate=pl.CostEstimate(flops=4 * 10**9, bytes_accessed=10**6, transcendentals=10**4),
    )(
        conn[0, 0], live[0], stiffness[0],
        owner.reshape(rows, LANES), free.reshape(rows, LANES),
        x_faces[0, 0], peer_table[0],
        disp.reshape(3 * rows, LANES), load.reshape(3 * rows, LANES),
        three_terms(forward), three_terms(backward),
    )
    return update.reshape(disp.shape), residual.reshape(disp.shape)


def solution(mesh):
    field = P("grp", "dom", None, None)
    flat = P("grp", "dom", None)
    in_specs = (field, flat, flat, flat, flat, field, flat, field, field)
    return jax.shard_map(
        functools.partial(per_device, mesh.shape["grp"], mesh.shape["dom"]),
        mesh=mesh, in_specs=in_specs, out_specs=(field, field), check_vma=False,
    )
```

```python
import functools
import math

import jax
import jax.numpy as jnp
import numpy as np
from jax import lax
from jax.experimental import pallas as pl
from jax.experimental.pallas import tpu as pltpu
from jax.sharding import PartitionSpec as P

MESH = pl.DeviceIdType.MESH
PZ = 8
LANES = 256
CHUNK = 128
UNROLL = 9
Q = 32
F32 = jnp.float32
BF16 = jnp.bfloat16
DIRECTIONS = (
    (0, -1, 640), (0, 1, 640), (-1, 0, 256), (1, 0, 256),
    (-1, -1, 128), (1, 1, 128), (-1, 1, 128), (1, -1, 128),
)
OPPOSITE = (1, 0, 3, 2, 5, 4, 7, 6)
STARTS = tuple(int(s) for s in np.cumsum([0] + [w for _, _, w in DIRECTIONS]))
DOM_WIDTH = STARTS[-1]


def lagrange_values(place):
    return np.array([place * (place - 1.0) / 2.0, 1.0 - place * place, place * (place + 1.0) / 2.0])


def lagrange_slopes(place):
    return np.array([place - 0.5, -2.0 * place, place + 0.5])


def basis_tables():
    points = [-math.sqrt(0.6), 0.0, math.sqrt(0.6)]
    weights = np.array([5.0 / 9.0, 8.0 / 9.0, 5.0 / 9.0])
    values = np.stack([lagrange_values(place) for place in points])
    slopes = np.stack([lagrange_slopes(place) for place in points])
    table = np.zeros((3, Q, Q))
    for d in range(3):
        factors = [slopes if d == k else values for k in range(3)]
        table[d, :27, :27] = np.einsum("ax,by,cz->abcxyz", *factors).reshape(27, 27)
    weight = np.einsum("a,b,c->abc", weights, weights, weights).reshape(27)
    forward = table.reshape(3 * Q, Q).copy()
    table[:, :27] *= weight[None, :, None]
    return forward, table.reshape(3 * Q, Q).T


def three_terms(table):
    table = np.asarray(table, np.float32)
    high = table.astype(BF16)
    low = (table - high.astype(np.float32)).astype(BF16)
    return jnp.asarray(np.concatenate([high, low, high], axis=1))


def halves(value):
    high = value.astype(BF16).astype(F32)
    return high, value - high


def stacked_halves(value):
    high, low = halves(value)
    return jnp.concatenate([high, low], axis=0).astype(BF16)


def one_hot(ids):
    spot = lax.broadcasted_iota(jnp.int32, (LANES, ids.shape[1]), 0)
    return jnp.where(spot == (ids & (LANES - 1)), 1.0, 0.0).astype(BF16)


def row_mask(ids, rows):
    spot = lax.broadcasted_iota(jnp.int32, (rows, ids.shape[1]), 0)
    return spot == (ids >> 8)


def pick(split_field, hot, ids):
    wide = jnp.dot(split_field, hot, preferred_element_type=F32)
    half = wide.shape[0] // 2
    wide = wide[:half] + wide[half:]
    rows = half // 3
    mask = row_mask(ids, rows)
    return [
        jnp.sum(jnp.where(mask, wide[c * rows : (c + 1) * rows], 0.0), axis=0, keepdims=True)
        for c in range(3)
    ]


def spread(values, hot, ids, rows):
    mask = row_mask(ids, rows)
    parts = [halves(value) for value in values]
    tall = jnp.concatenate([jnp.where(mask, parts[c][s], 0.0) for s in range(2) for c in range(3)], axis=0)
    total = lax.dot_general(
        tall.astype(BF16), hot, (((1,), (1,)), ((), ())), preferred_element_type=F32
    )
    return total


def cross(one, two):
    return [
        one[1] * two[2] - one[2] * two[1],
        one[2] * two[0] - one[0] * two[2],
        one[0] * two[1] - one[1] * two[0],
    ]


def kernel(
    n_grp, n_dom,
    conn, live, stiff, owner, free, faces, peers, disp, load, fwd, rev,
    update, residual,
    padded, hot_e, hot_x, hot_d, ids_x, ids_d, nodal, inverse, coef, force,
    send_x, recv_x, send_d, recv_d, dot_send, dot_dom, dot_grp,
    sx, rx, sd, rd, s_dot, r_dot, s_grp, r_grp,
):
    grp, dom = lax.axis_index("grp"), lax.axis_index("dom")
    py, pz = dom // PZ, lax.rem(dom, PZ)
    n_py = n_dom // PZ
    kept = owner.shape[0]
    rows = padded.shape[1] // 3
    slots = conn.shape[1]

    def exists(way):
        sy, sz, _ = DIRECTIONS[way]
        return (py + sy >= 0) & (py + sy < n_py) & (pz + sz >= 0) & (pz + sz < PZ)

    def peer(way):
        sy, sz, _ = DIRECTIONS[way]
        return jnp.clip(dom + sy * PZ + sz, 0, n_dom - 1)

    recv_x[...] = jnp.zeros_like(recv_x)
    recv_d[...] = jnp.zeros_like(recv_d)
    send_x[...] = jnp.zeros_like(send_x)
    send_d[...] = jnp.zeros_like(send_d)

    barrier = pltpu.get_barrier_semaphore()
    for k in range(1, n_dom):
        pl.semaphore_signal(barrier, inc=1, device_id={"dom": lax.rem(dom + k, n_dom)}, device_id_type=MESH)
    for k in range(1, n_grp):
        pl.semaphore_signal(barrier, inc=1, device_id={"grp": lax.rem(grp + k, n_grp)}, device_id_type=MESH)

    width_x = faces.shape[1]
    for side in range(2):
        ids_x[:, side * width_x : (side + 1) * width_x] = faces[side : side + 1, :]
    for way, (_, _, width) in enumerate(DIRECTIONS):
        ids_d[:, STARTS[way] : STARTS[way + 1]] = peers[pl.ds(peer(way), 1), :][:, :width]
    hot_x[...] = one_hot(ids_x[...])
    hot_d[...] = one_hot(ids_d[...])

    @pl.loop(0, 27)
    def _(a):
        hot_e[a] = one_hot(conn[pl.ds(a, 1), :])

    nodal[...] = jnp.zeros_like(nodal)
    padded[...] = jnp.zeros_like(padded)
    for c in range(3):
        here, there = pl.ds(c * kept, kept), pl.ds(c * rows, kept)
        padded[0, there, :] = owner[...].astype(F32)
        padded[1, there, :] = free[...].astype(F32)
        padded[2, there, :] = disp[here, :]
        padded[3, there, :] = load[here, :]
    own, loose = padded[0], padded[1]
    alive = live[...].astype(F32)
    shear = alive * stiff[...] / 2.6
    lame = alive * stiff[...] * 0.3 / 0.52

    pl.semaphore_wait(barrier, n_dom - 1 + n_grp - 1)

    def copy_x(turn, side):
        there = 1 - side
        return pltpu.make_async_remote_copy(
            src_ref=send_x.at[turn, :, pl.ds(side * width_x, width_x)],
            dst_ref=recv_x.at[turn, :, pl.ds(there * width_x, width_x)],
            send_sem=sx.at[turn, side],
            recv_sem=rx.at[turn, there],
            device_id={"grp": jnp.clip(grp + 2 * side - 1, 0, n_grp - 1)},
            device_id_type=MESH,
        )

    def copy_d(turn, way):
        there = OPPOSITE[way]
        width = DIRECTIONS[way][2]
        return pltpu.make_async_remote_copy(
            src_ref=send_d.at[turn, :, pl.ds(STARTS[way], width)],
            dst_ref=recv_d.at[turn, :, pl.ds(STARTS[there], width)],
            send_sem=sd.at[turn, way],
            recv_sem=rd.at[turn, there],
            device_id={"dom": peer(way)},
            device_id_type=MESH,
        )

    has_x = (grp > 0, grp < n_grp - 1)

    def added(total):
        half = total.shape[0] // 2
        return total[:half] + total[half:]

    def assemble(field, turn, between_x=None, between_d=None):
        picked = pick(stacked_halves(field), hot_x[...], ids_x[...])
        for c in range(3):
            send_x[turn, c : c + 1, :] = picked[c]
        for side in range(2):
            @pl.when(has_x[side])
            def _():
                copy_x(turn, side).start()
        if between_x is not None:
            between_x()
        for side in range(2):
            @pl.when(has_x[side])
            def _():
                copy_x(turn, side).wait_send()
                copy_x(turn, 1 - side).wait_recv()
        got = [recv_x[turn, c : c + 1, :] for c in range(3)]
        field = field + added(spread(got, hot_x[...], ids_x[...], rows))
        picked = pick(stacked_halves(field), hot_d[...], ids_d[...])
        for c in range(3):
            send_d[turn, c : c + 1, :] = picked[c]
        for way in range(8):
            @pl.when(exists(way))
            def _():
                copy_d(turn, way).start()
        if between_d is not None:
            between_d()
        for way in range(8):
            @pl.when(exists(way))
            def _():
                copy_d(turn, way).wait_send()
                copy_d(turn, OPPOSITE[way]).wait_recv()
        got = [recv_d[turn, c : c + 1, :] for c in range(3)]
        return field + added(spread(got, hot_d[...], ids_d[...], rows))

    def gradients(at):
        result = []
        for c in range(3):
            high, low = halves(nodal[c, :, at])
            stack = jnp.concatenate([high, high, low], axis=0).astype(BF16)
            full = jnp.dot(fwd[...], stack, preferred_element_type=F32)
            result.append([full[d * Q : (d + 1) * Q] for d in range(3)])
        return result

    def forces(field, tangent):
        split_field = stacked_halves(field)

        @pl.loop(0, 27 // UNROLL)
        def _(step):
            for part in range(UNROLL):
                a = step * UNROLL + part
                picked = pick(split_field, hot_e[a], conn[pl.ds(a, 1), :])
                for c in range(3):
                    nodal[c, pl.ds(a, 1), :] = picked[c]

        for first in range(0, slots, CHUNK):
            at = slice(first, first + CHUNK)
            mu, lam = shear[:, at], lame[:, at]
            change = gradients(at)
            if tangent:
                inv = [[inverse[3 * i + j, :, at] for j in range(3)] for i in range(3)]
                twist = coef[:, at]
                product = [
                    [sum(inv[i][k] * change[k][j] for k in range(3)) for j in range(3)] for i in range(3)
                ]
                trace = lam * (product[0][0] + product[1][1] + product[2][2])
                stress = [
                    [
                        mu * change[c][d]
                        + twist * sum(product[d][k] * inv[k][c] for k in range(3))
                        + trace * inv[d][c]
                        for d in range(3)
                    ]
                    for c in range(3)
                ]
            else:
                deform = [[change[c][d] + (1.0 if c == d else 0.0) for d in range(3)] for c in range(3)]
                columns = [
                    cross(deform[1], deform[2]), cross(deform[2], deform[0]), cross(deform[0], deform[1])
                ]
                volume = sum(deform[0][i] * columns[0][i] for i in range(3))
                over = 1.0 / volume
                logged = lam * jnp.log(volume)
                twist = mu - logged
                coef[:, at] = twist
                inv = [[columns[j][i] * over for j in range(3)] for i in range(3)]
                for i in range(3):
                    for j in range(3):
                        inverse[3 * i + j, :, at] = inv[i][j]
                stress = [[mu * deform[c][d] - twist * inv[d][c] for d in range(3)] for c in range(3)]
            for c in range(3):
                tall = jnp.concatenate(stress[c], axis=0)
                high, low = halves(tall)
                stack = jnp.concatenate([high, high, low], axis=0).astype(BF16)
                force[c, :, at] = jnp.dot(rev[...], stack, preferred_element_type=F32)

        def body(step, total):
            for part in range(UNROLL):
                a = step * UNROLL + part
                values = [force[c, pl.ds(a, 1), :] for c in range(3)]
                total = total + spread(values, hot_e[a], conn[pl.ds(a, 1), :], rows)
            return total

        return added(lax.fori_loop(0, 27 // UNROLL, body, jnp.zeros((6 * rows, LANES), F32)))

    state = assemble(own * padded[2], 0)
    inner = forces(state, False)
    right = loose * assemble(own * padded[3] - inner, 1)
    image = loose * assemble(forces(right, True), 2)
    second = forces(image, True)

    def lanes(value):
        return jnp.sum(value, axis=0, keepdims=True)

    partial = [
        lanes(own * right * right), lanes(own * right * image),
        lanes(own * image * image), lanes(image * second),
    ]
    dot_send[0] = jnp.concatenate(partial + [jnp.zeros((4, LANES), F32)], axis=0)

    def dot_copy(k):
        return pltpu.make_async_remote_copy(
            src_ref=dot_send.at[0], dst_ref=dot_dom.at[k], send_sem=s_dot.at[k], recv_sem=r_dot.at[k],
            device_id={"dom": lax.rem(dom + k, n_dom)}, device_id_type=MESH,
        )

    def grp_copy(k):
        return pltpu.make_async_remote_copy(
            src_ref=dot_send.at[1], dst_ref=dot_grp.at[k], send_sem=s_grp.at[k], recv_sem=r_grp.at[k],
            device_id={"grp": lax.rem(grp + k, n_grp)}, device_id_type=MESH,
        )

    def start_dots():
        for k in range(1, n_dom):
            dot_copy(k).start()

    def middle_dots():
        total = dot_send[0]
        for k in range(1, n_dom):
            dot_copy(k).wait()
            total = total + dot_dom[k]
        dot_send[1] = total
        for k in range(1, n_grp):
            grp_copy(k).start()

    outer = loose * assemble(second, 3, start_dots, middle_dots)
    total = dot_send[1]
    for k in range(1, n_grp):
        grp_copy(k).wait()
        total = total + dot_grp[k]
    sums = jnp.sum(total, axis=1, keepdims=True)
    rr, rq, qq, qu = (sums[k : k + 1] for k in range(4))
    step = rr / rq
    later = step * step * qq - rr
    ratio = later / rr
    grown = 1.0 + ratio
    curve = grown * grown * rq - 2.0 * grown * step * qq + step * step * qu
    last = later / curve
    moved = right - step * image
    direction = moved + ratio * right
    padded[2] = step * right + last * direction
    padded[3] = moved - last * (grown * image - step * outer)
    for c in range(3):
        here, there = pl.ds(c * kept, kept), pl.ds(c * rows, kept)
        update[here, :] = padded[2, there, :]
        residual[here, :] = padded[3, there, :]


def per_device(n_grp, n_dom, conn, live, stiffness, owner, free, x_faces, peer_table, disp, load):
    slots = conn.shape[3]
    rows = owner.shape[2] // LANES
    width_x = x_faces.shape[3]
    forward, backward = basis_tables()
    vmem = pl.BlockSpec(memory_space=pltpu.VMEM)
    shape = jax.ShapeDtypeStruct((3 * rows, LANES), F32)
    dma = pltpu.SemaphoreType.DMA
    update, residual = pl.pallas_call(
        functools.partial(kernel, n_grp, n_dom),
        out_shape=(shape, shape),
        in_specs=[vmem] * 11,
        out_specs=(vmem, vmem),
        scratch_shapes=[
            pltpu.VMEM((4, 3 * (-(-rows // 8) * 8), LANES), F32),
            pltpu.VMEM((27, LANES, slots), BF16),
            pltpu.VMEM((LANES, 2 * width_x), BF16),
            pltpu.VMEM((LANES, DOM_WIDTH), BF16),
            pltpu.VMEM((1, 2 * width_x), jnp.int32),
            pltpu.VMEM((1, DOM_WIDTH), jnp.int32),
            pltpu.VMEM((3, Q, slots), F32),
            pltpu.VMEM((9, Q, slots), F32),
            pltpu.VMEM((Q, slots), F32),
            pltpu.VMEM((3, Q, slots), F32),
            pltpu.VMEM((4, 8, 2 * width_x), F32),
            pltpu.VMEM((4, 8, 2 * width_x), F32),
            pltpu.VMEM((4, 8, DOM_WIDTH), F32),
            pltpu.VMEM((4, 8, DOM_WIDTH), F32),
            pltpu.VMEM((2, 8, LANES), F32),
            pltpu.VMEM((n_dom, 8, LANES), F32),
            pltpu.VMEM((n_grp, 8, LANES), F32),
            dma((4, 2)), dma((4, 2)), dma((4, 8)), dma((4, 8)),
            dma((n_dom,)), dma((n_dom,)), dma((n_grp,)), dma((n_grp,)),
        ],
        compiler_params=pltpu.CompilerParams(
            collective_id=0, has_side_effects=True, vmem_limit_bytes=48 * 1024 * 1024
        ),
        cost_estimate=pl.CostEstimate(flops=4 * 10**9, bytes_accessed=10**6, transcendentals=10**4),
    )(
        conn[0, 0], live[0], stiffness[0],
        owner.reshape(rows, LANES), free.reshape(rows, LANES),
        x_faces[0, 0], peer_table[0],
        disp.reshape(3 * rows, LANES), load.reshape(3 * rows, LANES),
        three_terms(forward), three_terms(backward),
    )
    return update.reshape(disp.shape), residual.reshape(disp.shape)


def solution(mesh):
    field = P("grp", "dom", None, None)
    flat = P("grp", "dom", None)
    in_specs = (field, flat, flat, flat, flat, field, flat, field, field)
    return jax.shard_map(
        functools.partial(per_device, mesh.shape["grp"], mesh.shape["dom"]),
        mesh=mesh, in_specs=in_specs, out_specs=(field, field), check_vma=False,
    )
```

```python
import functools
import math

import jax
import jax.numpy as jnp
import numpy as np
from jax import lax
from jax.experimental import pallas as pl
from jax.experimental.pallas import tpu as pltpu
from jax.sharding import PartitionSpec as P

MESH = pl.DeviceIdType.MESH
PZ = 8
LANES = 256
CHUNK = 128
GATHER_UNROLL = 27
SCATTER_UNROLL = 9
Q = 32
F32 = jnp.float32
BF16 = jnp.bfloat16
DIRECTIONS = (
    (0, -1, 640), (0, 1, 640), (-1, 0, 256), (1, 0, 256),
    (-1, -1, 128), (1, 1, 128), (-1, 1, 128), (1, -1, 128),
)
OPPOSITE = (1, 0, 3, 2, 5, 4, 7, 6)
STARTS = tuple(int(s) for s in np.cumsum([0] + [w for _, _, w in DIRECTIONS]))
DOM_WIDTH = STARTS[-1]


def lagrange_values(place):
    return np.array([place * (place - 1.0) / 2.0, 1.0 - place * place, place * (place + 1.0) / 2.0])


def lagrange_slopes(place):
    return np.array([place - 0.5, -2.0 * place, place + 0.5])


def basis_tables():
    points = [-math.sqrt(0.6), 0.0, math.sqrt(0.6)]
    weights = np.array([5.0 / 9.0, 8.0 / 9.0, 5.0 / 9.0])
    values = np.stack([lagrange_values(place) for place in points])
    slopes = np.stack([lagrange_slopes(place) for place in points])
    table = np.zeros((3, Q, Q))
    for d in range(3):
        factors = [slopes if d == k else values for k in range(3)]
        table[d, :27, :27] = np.einsum("ax,by,cz->abcxyz", *factors).reshape(27, 27)
    weight = np.einsum("a,b,c->abc", weights, weights, weights).reshape(27)
    forward = table.reshape(3 * Q, Q).copy()
    table[:, :27] *= weight[None, :, None]
    return forward, table.reshape(3 * Q, Q).T


def three_terms(table):
    table = np.asarray(table, np.float32)
    high = table.astype(BF16)
    low = (table - high.astype(np.float32)).astype(BF16)
    return jnp.asarray(np.concatenate([high, low, high], axis=1))


def halves(value):
    high = value.astype(BF16).astype(F32)
    return high, value - high


def stacked_halves(value):
    high, low = halves(value)
    return jnp.concatenate([high, low], axis=0).astype(BF16)


def one_hot(ids):
    spot = lax.broadcasted_iota(jnp.int32, (LANES, ids.shape[1]), 0)
    return jnp.where(spot == (ids & (LANES - 1)), 1.0, 0.0).astype(BF16)


def row_mask(ids, rows):
    spot = lax.broadcasted_iota(jnp.int32, (rows, ids.shape[1]), 0)
    return spot == (ids >> 8)


def pick(split_field, hot, ids):
    wide = jnp.dot(split_field, hot, preferred_element_type=F32)
    half = wide.shape[0] // 2
    wide = wide[:half] + wide[half:]
    rows = half // 3
    mask = row_mask(ids, rows)
    return [
        jnp.sum(jnp.where(mask, wide[c * rows : (c + 1) * rows], 0.0), axis=0, keepdims=True)
        for c in range(3)
    ]


def spread(values, hot, ids, rows):
    mask = row_mask(ids, rows)
    parts = [halves(value) for value in values]
    tall = jnp.concatenate([jnp.where(mask, parts[c][s], 0.0) for s in range(2) for c in range(3)], axis=0)
    total = lax.dot_general(
        tall.astype(BF16), hot, (((1,), (1,)), ((), ())), preferred_element_type=F32
    )
    return total


def cross(one, two):
    return [
        one[1] * two[2] - one[2] * two[1],
        one[2] * two[0] - one[0] * two[2],
        one[0] * two[1] - one[1] * two[0],
    ]


def kernel(
    n_grp, n_dom,
    conn, live, stiff, owner, free, faces, peers, disp, load, fwd, rev,
    update, residual,
    padded, hot_e, hot_x, hot_d, ids_x, ids_d, nodal, inverse, coef, force,
    send_x, recv_x, send_d, recv_d, dot_send, dot_dom, dot_grp,
    sx, rx, sd, rd, s_dot, r_dot, s_grp, r_grp,
):
    grp, dom = lax.axis_index("grp"), lax.axis_index("dom")
    py, pz = dom // PZ, lax.rem(dom, PZ)
    n_py = n_dom // PZ
    kept = owner.shape[0]
    rows = padded.shape[1] // 3
    slots = conn.shape[1]

    def exists(way):
        sy, sz, _ = DIRECTIONS[way]
        return (py + sy >= 0) & (py + sy < n_py) & (pz + sz >= 0) & (pz + sz < PZ)

    def peer(way):
        sy, sz, _ = DIRECTIONS[way]
        return jnp.clip(dom + sy * PZ + sz, 0, n_dom - 1)

    recv_x[...] = jnp.zeros_like(recv_x)
    recv_d[...] = jnp.zeros_like(recv_d)
    send_x[...] = jnp.zeros_like(send_x)
    send_d[...] = jnp.zeros_like(send_d)

    barrier = pltpu.get_barrier_semaphore()
    for k in range(1, n_dom):
        pl.semaphore_signal(barrier, inc=1, device_id={"dom": lax.rem(dom + k, n_dom)}, device_id_type=MESH)
    for k in range(1, n_grp):
        pl.semaphore_signal(barrier, inc=1, device_id={"grp": lax.rem(grp + k, n_grp)}, device_id_type=MESH)

    width_x = faces.shape[1]
    for side in range(2):
        ids_x[:, side * width_x : (side + 1) * width_x] = faces[side : side + 1, :]
    for way, (_, _, width) in enumerate(DIRECTIONS):
        ids_d[:, STARTS[way] : STARTS[way + 1]] = peers[pl.ds(peer(way), 1), :][:, :width]
    hot_x[...] = one_hot(ids_x[...])
    hot_d[...] = one_hot(ids_d[...])

    @pl.loop(0, 27)
    def _(a):
        hot_e[a] = one_hot(conn[pl.ds(a, 1), :])

    nodal[...] = jnp.zeros_like(nodal)
    padded[...] = jnp.zeros_like(padded)
    for c in range(3):
        here, there = pl.ds(c * kept, kept), pl.ds(c * rows, kept)
        padded[0, there, :] = owner[...].astype(F32)
        padded[1, there, :] = free[...].astype(F32)
        padded[2, there, :] = disp[here, :]
        padded[3, there, :] = load[here, :]
    own, loose = padded[0], padded[1]
    alive = live[...].astype(F32)
    shear = alive * stiff[...] / 2.6
    lame = alive * stiff[...] * 0.3 / 0.52

    pl.semaphore_wait(barrier, n_dom - 1 + n_grp - 1)

    def copy_x(turn, side):
        there = 1 - side
        return pltpu.make_async_remote_copy(
            src_ref=send_x.at[turn, :, pl.ds(side * width_x, width_x)],
            dst_ref=recv_x.at[turn, :, pl.ds(there * width_x, width_x)],
            send_sem=sx.at[turn, side],
            recv_sem=rx.at[turn, there],
            device_id={"grp": jnp.clip(grp + 2 * side - 1, 0, n_grp - 1)},
            device_id_type=MESH,
        )

    def copy_d(turn, way):
        there = OPPOSITE[way]
        width = DIRECTIONS[way][2]
        return pltpu.make_async_remote_copy(
            src_ref=send_d.at[turn, :, pl.ds(STARTS[way], width)],
            dst_ref=recv_d.at[turn, :, pl.ds(STARTS[there], width)],
            send_sem=sd.at[turn, way],
            recv_sem=rd.at[turn, there],
            device_id={"dom": peer(way)},
            device_id_type=MESH,
        )

    has_x = (grp > 0, grp < n_grp - 1)

    def added(total):
        half = total.shape[0] // 2
        return total[:half] + total[half:]

    def assemble(field, turn, between_x=None, between_d=None):
        picked = pick(stacked_halves(field), hot_x[...], ids_x[...])
        for c in range(3):
            send_x[turn, c : c + 1, :] = picked[c]
        for side in range(2):
            @pl.when(has_x[side])
            def _():
                copy_x(turn, side).start()
        if between_x is not None:
            between_x()
        for side in range(2):
            @pl.when(has_x[side])
            def _():
                copy_x(turn, side).wait_send()
                copy_x(turn, 1 - side).wait_recv()
        got = [recv_x[turn, c : c + 1, :] for c in range(3)]
        field = field + added(spread(got, hot_x[...], ids_x[...], rows))
        picked = pick(stacked_halves(field), hot_d[...], ids_d[...])
        for c in range(3):
            send_d[turn, c : c + 1, :] = picked[c]
        for way in range(8):
            @pl.when(exists(way))
            def _():
                copy_d(turn, way).start()
        if between_d is not None:
            between_d()
        for way in range(8):
            @pl.when(exists(way))
            def _():
                copy_d(turn, way).wait_send()
                copy_d(turn, OPPOSITE[way]).wait_recv()
        got = [recv_d[turn, c : c + 1, :] for c in range(3)]
        return field + added(spread(got, hot_d[...], ids_d[...], rows))

    def gradients(at):
        result = []
        for c in range(3):
            high, low = halves(nodal[c, :, at])
            stack = jnp.concatenate([high, high, low], axis=0).astype(BF16)
            full = jnp.dot(fwd[...], stack, preferred_element_type=F32)
            result.append([full[d * Q : (d + 1) * Q] for d in range(3)])
        return result

    def forces(field, tangent):
        split_field = stacked_halves(field)

        @pl.loop(0, 27 // GATHER_UNROLL)
        def _(step):
            for part in range(GATHER_UNROLL):
                a = step * GATHER_UNROLL + part
                picked = pick(split_field, hot_e[a], conn[pl.ds(a, 1), :])
                for c in range(3):
                    nodal[c, pl.ds(a, 1), :] = picked[c]

        for first in range(0, slots, CHUNK):
            at = slice(first, first + CHUNK)
            mu, lam = shear[:, at], lame[:, at]
            change = gradients(at)
            if tangent:
                inv = [[inverse[3 * i + j, :, at] for j in range(3)] for i in range(3)]
                twist = coef[:, at]
                product = [
                    [sum(inv[i][k] * change[k][j] for k in range(3)) for j in range(3)] for i in range(3)
                ]
                trace = lam * (product[0][0] + product[1][1] + product[2][2])
                stress = [
                    [
                        mu * change[c][d]
                        + twist * sum(product[d][k] * inv[k][c] for k in range(3))
                        + trace * inv[d][c]
                        for d in range(3)
                    ]
                    for c in range(3)
                ]
            else:
                deform = [[change[c][d] + (1.0 if c == d else 0.0) for d in range(3)] for c in range(3)]
                columns = [
                    cross(deform[1], deform[2]), cross(deform[2], deform[0]), cross(deform[0], deform[1])
                ]
                volume = sum(deform[0][i] * columns[0][i] for i in range(3))
                over = 1.0 / volume
                logged = lam * jnp.log(volume)
                twist = mu - logged
                coef[:, at] = twist
                inv = [[columns[j][i] * over for j in range(3)] for i in range(3)]
                for i in range(3):
                    for j in range(3):
                        inverse[3 * i + j, :, at] = inv[i][j]
                stress = [[mu * deform[c][d] - twist * inv[d][c] for d in range(3)] for c in range(3)]
            for c in range(3):
                tall = jnp.concatenate(stress[c], axis=0)
                high, low = halves(tall)
                stack = jnp.concatenate([high, high, low], axis=0).astype(BF16)
                force[c, :, at] = jnp.dot(rev[...], stack, preferred_element_type=F32)

        def body(step, total):
            for part in range(SCATTER_UNROLL):
                a = step * SCATTER_UNROLL + part
                values = [force[c, pl.ds(a, 1), :] for c in range(3)]
                total = total + spread(values, hot_e[a], conn[pl.ds(a, 1), :], rows)
            return total

        return added(lax.fori_loop(0, 27 // SCATTER_UNROLL, body, jnp.zeros((6 * rows, LANES), F32)))

    state = assemble(own * padded[2], 0)
    inner = forces(state, False)
    right = loose * assemble(own * padded[3] - inner, 1)
    image = loose * assemble(forces(right, True), 2)
    second = forces(image, True)

    def lanes(value):
        return jnp.sum(value, axis=0, keepdims=True)

    partial = [
        lanes(own * right * right), lanes(own * right * image),
        lanes(own * image * image), lanes(image * second),
    ]
    dot_send[0] = jnp.concatenate(partial + [jnp.zeros((4, LANES), F32)], axis=0)

    def dot_copy(k):
        return pltpu.make_async_remote_copy(
            src_ref=dot_send.at[0], dst_ref=dot_dom.at[k], send_sem=s_dot.at[k], recv_sem=r_dot.at[k],
            device_id={"dom": lax.rem(dom + k, n_dom)}, device_id_type=MESH,
        )

    def grp_copy(k):
        return pltpu.make_async_remote_copy(
            src_ref=dot_send.at[1], dst_ref=dot_grp.at[k], send_sem=s_grp.at[k], recv_sem=r_grp.at[k],
            device_id={"grp": lax.rem(grp + k, n_grp)}, device_id_type=MESH,
        )

    def start_dots():
        for k in range(1, n_dom):
            dot_copy(k).start()

    def middle_dots():
        total = dot_send[0]
        for k in range(1, n_dom):
            dot_copy(k).wait()
            total = total + dot_dom[k]
        dot_send[1] = total
        for k in range(1, n_grp):
            grp_copy(k).start()

    outer = loose * assemble(second, 3, start_dots, middle_dots)
    total = dot_send[1]
    for k in range(1, n_grp):
        grp_copy(k).wait()
        total = total + dot_grp[k]
    sums = jnp.sum(total, axis=1, keepdims=True)
    rr, rq, qq, qu = (sums[k : k + 1] for k in range(4))
    step = rr / rq
    later = step * step * qq - rr
    ratio = later / rr
    grown = 1.0 + ratio
    curve = grown * grown * rq - 2.0 * grown * step * qq + step * step * qu
    last = later / curve
    moved = right - step * image
    direction = moved + ratio * right
    padded[2] = step * right + last * direction
    padded[3] = moved - last * (grown * image - step * outer)
    for c in range(3):
        here, there = pl.ds(c * kept, kept), pl.ds(c * rows, kept)
        update[here, :] = padded[2, there, :]
        residual[here, :] = padded[3, there, :]


def per_device(n_grp, n_dom, conn, live, stiffness, owner, free, x_faces, peer_table, disp, load):
    slots = conn.shape[3]
    rows = owner.shape[2] // LANES
    width_x = x_faces.shape[3]
    forward, backward = basis_tables()
    vmem = pl.BlockSpec(memory_space=pltpu.VMEM)
    shape = jax.ShapeDtypeStruct((3 * rows, LANES), F32)
    dma = pltpu.SemaphoreType.DMA
    update, residual = pl.pallas_call(
        functools.partial(kernel, n_grp, n_dom),
        out_shape=(shape, shape),
        in_specs=[vmem] * 11,
        out_specs=(vmem, vmem),
        scratch_shapes=[
            pltpu.VMEM((4, 3 * (-(-rows // 8) * 8), LANES), F32),
            pltpu.VMEM((27, LANES, slots), BF16),
            pltpu.VMEM((LANES, 2 * width_x), BF16),
            pltpu.VMEM((LANES, DOM_WIDTH), BF16),
            pltpu.VMEM((1, 2 * width_x), jnp.int32),
            pltpu.VMEM((1, DOM_WIDTH), jnp.int32),
            pltpu.VMEM((3, Q, slots), F32),
            pltpu.VMEM((9, Q, slots), F32),
            pltpu.VMEM((Q, slots), F32),
            pltpu.VMEM((3, Q, slots), F32),
            pltpu.VMEM((4, 8, 2 * width_x), F32),
            pltpu.VMEM((4, 8, 2 * width_x), F32),
            pltpu.VMEM((4, 8, DOM_WIDTH), F32),
            pltpu.VMEM((4, 8, DOM_WIDTH), F32),
            pltpu.VMEM((2, 8, LANES), F32),
            pltpu.VMEM((n_dom, 8, LANES), F32),
            pltpu.VMEM((n_grp, 8, LANES), F32),
            dma((4, 2)), dma((4, 2)), dma((4, 8)), dma((4, 8)),
            dma((n_dom,)), dma((n_dom,)), dma((n_grp,)), dma((n_grp,)),
        ],
        compiler_params=pltpu.CompilerParams(
            collective_id=0, has_side_effects=True, vmem_limit_bytes=48 * 1024 * 1024
        ),
        cost_estimate=pl.CostEstimate(flops=4 * 10**9, bytes_accessed=10**6, transcendentals=10**4),
    )(
        conn[0, 0], live[0], stiffness[0],
        owner.reshape(rows, LANES), free.reshape(rows, LANES),
        x_faces[0, 0], peer_table[0],
        disp.reshape(3 * rows, LANES), load.reshape(3 * rows, LANES),
        three_terms(forward), three_terms(backward),
    )
    return update.reshape(disp.shape), residual.reshape(disp.shape)


def solution(mesh):
    field = P("grp", "dom", None, None)
    flat = P("grp", "dom", None)
    in_specs = (field, flat, flat, flat, flat, field, flat, field, field)
    return jax.shard_map(
        functools.partial(per_device, mesh.shape["grp"], mesh.shape["dom"]),
        mesh=mesh, in_specs=in_specs, out_specs=(field, field), check_vma=False,
    )
```
